32 devices in a mesh: tm: 16 (over z, y, x), rep: 2 (over core).
Axes of the slice: x: 2, y: 2, z: 4, core: 2. Of those that a mesh axis runs over, the one named last changes fastest.
Arguments:
- table: bfloat16 [2, 4096, 512], P(None, 'tm'), may hold values from -30 to 30
- cotangent: bfloat16 [2, 4096, 512], P(None, 'tm'), may hold values from -6 to 6
- stamps: int32 [2, 4096], P(None, 'tm'), may hold values from 0 to 12288, as said below
- starts: int32 [2, 4096], P(None, 'tm'), may hold values from 0 to 8191, as said below
- w_query: bfloat16 [512, 512], P(None, 'rep'), may hold values from -0.5 to 0.5
- w_key: bfloat16 [512, 512], P(None, 'rep'), may hold values from -0.5 to 0.5
- w_value: bfloat16 [512, 512], P(None, 'rep'), may hold values from -0.25 to 0.25
- w_out: bfloat16 [512, 512], P('rep'), may hold values from -0.25 to 0.25
- decay: float32 [4], P('rep'), may hold values from 0.0002 to 0.02
Outputs:
- mixed: bfloat16 [2, 4096, 512], P(None, 'tm')
- grad_table: bfloat16 [2, 4096, 512], P(None, 'tm')
- grad_query: float32 [512, 512], P(None, 'rep')
- grad_key: float32 [512, 512], P(None, 'rep')
- grad_value: float32 [512, 512], P(None, 'rep')
- grad_out: float32 [512, 512], P('rep')
The draws below stay inside these ranges and needn't reach their ends.
Inputs may be any that keep to these rules, and one draw needn't show every extreme that they name: In time order the stamps never fall, successive rows differ by 0 to 3, the first row has stamp 0 and the last row has stamp 3 * 4096. For the row r in time order, starts lies between max(0, (r // 256 - 2) * 256) and r; the first row of each block reaches the lower end and the last row of each block starts at itself.
All inputs are finite; a program needn't handle non-finite values.
Results may differ from the reference program's by a relative error of at most 0.0045.
The reference program's roundings to bfloat16 on the way count: a program that leaves them out, or rounds other values in their place, can miss the bound.
Values may be sent and summed in bfloat16 or wider, within the bound.
No kernel may reach another device: no remote copies, remote signals or barrier semaphores. Data moves between devices by JAX's collectives and lax.ppermute only.
A program may use at most 64 MiB of HBM per device.

```python
import math
import jax
import jax.numpy as jnp
from jax import lax

D = 512
HEADS = 4
HD = 128
BLK = 256
ROWS = 8192


def fold_rows(ordered):
    tail = ordered.shape[1:]
    half = ROWS // (2 * BLK)
    blocks = ordered.reshape((2 * half, BLK) + tail)
    lower = blocks[:half].reshape((half * BLK,) + tail)
    upper = blocks[half:][::-1].reshape((half * BLK,) + tail)
    return jnp.stack([lower, upper])


def draw_table(key, part):
    noise = jax.random.normal(jax.random.fold_in(key, 1), (ROWS, D), jnp.float32)
    noise = jnp.clip(noise, -6.0, 6.0)
    return fold_rows(noise).astype(jnp.bfloat16)


def weight_pair(key):
    base = jax.random.normal(jax.random.fold_in(key, 31), (D, D), jnp.float32) / math.sqrt(D)
    other = jax.random.normal(jax.random.fold_in(key, 32), (D, D), jnp.float32) / math.sqrt(D)
    paired = other
    return (jnp.clip(base, -0.5, 0.5), jnp.clip(paired, -0.5, 0.5))


def draw_w_query(key, part):
    return weight_pair(key)[0].astype(jnp.bfloat16)


def draw_w_key(key, part):
    return weight_pair(key)[1].astype(jnp.bfloat16)


def draw_stamps(key, part):
    pair_count = ROWS // 2 - 1
    firsts = jax.random.randint(jax.random.fold_in(key, 41), (pair_count,), 0, 4, dtype=jnp.int32)
    paired = jnp.stack([firsts, 3 - firsts], 1).reshape(2 * pair_count)
    gaps = jnp.concatenate([jnp.full((1,), 3, jnp.int32), paired, jnp.zeros((1,), jnp.int32)])
    times = jnp.cumsum(gaps).astype(jnp.int32) - gaps
    return fold_rows(times)


def draw_starts(key, part):
    row_ids = jnp.arange(ROWS, dtype=jnp.int32)
    blk_ids = row_ids // BLK
    lowest = jnp.maximum(0, (blk_ids - 2) * BLK)
    span = row_ids - lowest
    modes = jax.random.randint(jax.random.fold_in(key, 51), (ROWS // BLK,), 0, 3, dtype=jnp.int32)[blk_ids]
    raw = jax.random.randint(jax.random.fold_in(key, 52), (ROWS,), 0, 1 << 20, dtype=jnp.int32)
    short = raw % jnp.minimum(span + 1, 48)
    spread = raw % (span + 1)
    back = jnp.where(modes == 0, short, jnp.where(modes == 1, spread, span))
    back = jnp.where(row_ids % BLK == 0, span, back)
    back = jnp.where(row_ids % BLK == BLK - 1, 0, back)
    return fold_rows((row_ids - back).astype(jnp.int32))


def level_of(rng, extent, cuts, least, high):
    loudness = 1.0
    for dim, shards_of in cuts:
        heights = jax.random.uniform(jax.random.fold_in(jax.random.fold_in(rng, 6), dim), (shards_of,), jnp.float32, least / len(cuts), high / len(cuts))
        loudness = loudness * jnp.repeat(jnp.exp(heights), extent[dim] // shards_of).reshape((-1,) + (1,) * (len(extent) - 1 - dim))
    return loudness


def gaussian(stream_key, shape, scale, reach, shards=(), kind=jnp.bfloat16):
    values = scale * jax.random.normal(stream_key, shape, jnp.float32)
    if shards:
        values = values * level_of(stream_key, shape, shards, -0.22, 0.18)
    return jnp.clip(values, -reach, reach).astype(kind)


def setup_inputs(seed: int = 0) -> dict:
    arg_keys = jax.random.split(jax.random.key(seed), 10)
    table = draw_table(jax.random.fold_in(arg_keys[9], 71), 0)
    cotangent = gaussian(arg_keys[1], (2, ROWS // 2, D), 1.0, 6.0, ((1, 16),))
    stamps = draw_stamps(jax.random.fold_in(arg_keys[9], 71), 0)
    starts = draw_starts(jax.random.fold_in(arg_keys[9], 71), 0)
    w_query = draw_w_query(jax.random.fold_in(arg_keys[9], 71), 0)
    w_key = draw_w_key(jax.random.fold_in(arg_keys[9], 71), 0)
    w_value = gaussian(arg_keys[6], (D, D), D ** -0.5, 0.25, ((1, 2),))
    w_out = gaussian(arg_keys[7], (D, D), D ** -0.5, 0.25, ((0, 2),))
    decay = jnp.clip(jnp.exp(math.log(0.02) - 4.6051702 * jax.random.uniform(arg_keys[8], (HEADS,), jnp.float32) ** level_of(arg_keys[8], (HEADS,), ((0, 2),), -0.2, 0.2)), 0.0002, 0.02)
    return {"table": table, "cotangent": cotangent, "stamps": stamps, "starts": starts, "w_query": w_query, "w_key": w_key, "w_value": w_value, "w_out": w_out, "decay": decay}


def unfold(folded):
    tail = folded.shape[2:]
    half = folded.shape[1] // BLK
    lower = folded[0].reshape((half, BLK) + tail)
    upper = folded[1].reshape((half, BLK) + tail)[::-1]
    return jnp.concatenate([lower, upper], 0).reshape((2 * half * BLK,) + tail)

def fold_back(ordered):
    tail = ordered.shape[1:]
    half = ordered.shape[0] // (2 * BLK)
    blocks = ordered.reshape((2 * half, BLK) + tail)
    lower = blocks[:half].reshape((half * BLK,) + tail)
    upper = blocks[half:][::-1].reshape((half * BLK,) + tail)
    return jnp.stack([lower, upper])

def reference(table, cotangent, stamps, starts, w_query, w_key, w_value, w_out, decay):
    rows = unfold(table)
    grad_y = unfold(cotangent)
    times = unfold(stamps)
    firsts = unfold(starts)
    total = rows.shape[0]
    blocks_all = total // BLK
    queries = jnp.dot(rows, w_query, preferred_element_type=jnp.float32).astype(jnp.bfloat16)
    key_rows = jnp.dot(rows, w_key, preferred_element_type=jnp.float32).astype(jnp.bfloat16)
    val_rows = jnp.dot(rows, w_value, preferred_element_type=jnp.float32).astype(jnp.bfloat16)
    grad_attn = jnp.dot(grad_y, w_out.T, preferred_element_type=jnp.float32).astype(jnp.bfloat16)
    inv_scale = 1.0 / math.sqrt(HD)
    margin = 2 * BLK
    key_pad = jnp.pad(key_rows, ((margin, 0), (0, 0)))
    val_pad = jnp.pad(val_rows, ((margin, 0), (0, 0)))
    time_pad = jnp.pad(times, (margin, 0))

    def step(carry, blk_id):
        key_acc, val_acc = carry
        row_zero = blk_id * BLK
        q_heads = lax.dynamic_slice_in_dim(queries, row_zero, BLK, 0).reshape(BLK, HEADS, HD).astype(jnp.float32)
        k_heads = lax.dynamic_slice_in_dim(key_pad, row_zero, 3 * BLK, 0).reshape(3 * BLK, HEADS, HD).astype(jnp.float32)
        v_heads = lax.dynamic_slice_in_dim(val_pad, row_zero, 3 * BLK, 0).reshape(3 * BLK, HEADS, HD).astype(jnp.float32)
        g_heads = lax.dynamic_slice_in_dim(grad_attn, row_zero, BLK, 0).reshape(BLK, HEADS, HD).astype(jnp.float32)
        q_times = lax.dynamic_slice_in_dim(times, row_zero, BLK, 0)
        k_times = lax.dynamic_slice_in_dim(time_pad, row_zero, 3 * BLK, 0)
        q_first = lax.dynamic_slice_in_dim(firsts, row_zero, BLK, 0)
        q_pos = row_zero + jnp.arange(BLK, dtype=jnp.int32)
        k_pos = row_zero - margin + jnp.arange(3 * BLK, dtype=jnp.int32)
        allowed = (k_pos[None, :] >= q_first[:, None]) & (k_pos[None, :] <= q_pos[:, None])
        time_gap = (q_times[:, None] - k_times[None, :]).astype(jnp.float32)
        scores = jnp.einsum('qhd,khd->hqk', q_heads, k_heads) * inv_scale - decay[:, None, None] * time_gap[None]
        scores = jnp.where(allowed[None], scores, -1e+30)
        row_max = lax.optimization_barrier(jnp.max(scores, -1, keepdims=True))
        weights = jnp.where(allowed[None], jnp.exp(scores - row_max), 0.0)
        probs = weights / lax.optimization_barrier(jnp.sum(weights, -1, keepdims=True))
        probs_low = probs.astype(jnp.bfloat16).astype(jnp.float32)
        attn = jnp.einsum('hqk,khd->qhd', probs_low, v_heads).astype(jnp.bfloat16)
        d_probs = jnp.einsum('qhd,khd->hqk', g_heads, v_heads)
        delta = lax.optimization_barrier(jnp.sum(probs * d_probs, -1, keepdims=True))
        d_scores = (probs * (d_probs - delta)).astype(jnp.bfloat16).astype(jnp.float32)
        d_query = (jnp.einsum('hqk,khd->qhd', d_scores, k_heads) * inv_scale).astype(jnp.bfloat16)
        d_key = jnp.einsum('hqk,qhd->khd', d_scores, q_heads) * inv_scale
        d_value = jnp.einsum('hqk,qhd->khd', probs_low, g_heads)
        old_key = lax.dynamic_slice_in_dim(key_acc, row_zero, 3 * BLK, 0)
        key_acc = lax.dynamic_update_slice_in_dim(key_acc, old_key + d_key.reshape(3 * BLK, D), row_zero, 0)
        old_val = lax.dynamic_slice_in_dim(val_acc, row_zero, 3 * BLK, 0)
        val_acc = lax.dynamic_update_slice_in_dim(val_acc, old_val + d_value.reshape(3 * BLK, D), row_zero, 0)
        return ((key_acc, val_acc), (attn.reshape(BLK, D), d_query.reshape(BLK, D)))
    zero_acc = jnp.zeros((total + margin, D), jnp.float32)
    (key_acc, val_acc), (attn_blocks, dq_blocks) = lax.scan(step, (zero_acc, zero_acc), jnp.arange(blocks_all, dtype=jnp.int32))
    attn_all = attn_blocks.reshape(total, D)
    dq_all = dq_blocks.reshape(total, D)
    dk_all = key_acc[margin:].astype(jnp.bfloat16)
    dv_all = val_acc[margin:].astype(jnp.bfloat16)
    mixed = jnp.dot(attn_all, w_out, preferred_element_type=jnp.float32).astype(jnp.bfloat16)
    grad_rows = (jnp.dot(dq_all, w_query.T, preferred_element_type=jnp.float32) + jnp.dot(dk_all, w_key.T, preferred_element_type=jnp.float32) + jnp.dot(dv_all, w_value.T, preferred_element_type=jnp.float32)).astype(jnp.bfloat16)
    grad_scale = 1.0 / math.sqrt(total)
    grad_query = jnp.dot(rows.T, dq_all, preferred_element_type=jnp.float32) * grad_scale
    grad_key = jnp.dot(rows.T, dk_all, preferred_element_type=jnp.float32) * grad_scale
    grad_value = jnp.dot(rows.T, dv_all, preferred_element_type=jnp.float32) * grad_scale
    grad_out = jnp.dot(attn_all.T, grad_y, preferred_element_type=jnp.float32) * grad_scale
    return (fold_back(mixed), fold_back(grad_rows), grad_query, grad_key, grad_value, grad_out)
```

```python
import functools
import math

import jax
import jax.numpy as jnp
from jax import lax
from jax.experimental import pallas as pl
from jax.experimental.pallas import tpu as pltpu
from jax.sharding import PartitionSpec as P

HD = 128
BF = jnp.bfloat16
F32 = jnp.float32
AXES = ("tm", "rep")
LOG2E = math.log2(math.e)


def dot(a, b, dims=((1,), (0,))):
    return lax.dot_general(a, b, (dims, ((), ())), preferred_element_type=F32)


def swap_cores(x):
    return lax.ppermute(x, "rep", [(0, 1), (1, 0)])


def shift_blocks(x, distance):
    n = lax.axis_size("tm")

    def worker(b):
        return 2 * b if b < n else 2 * (2 * n - 1 - b) + 1

    route = [(worker(b), worker((b + distance) % (2 * n))) for b in range(2 * n)]
    return lax.ppermute(x, AXES, route)


def bit_orders():
    bits = lax.axis_size("tm").bit_length() - 1
    count = min(3, bits)
    first = list(range(count))
    return first, first[-1:] + first[:-1], list(range(count, bits))


def partners(bit0, bit1):
    n = lax.axis_size("tm")
    pairs = []
    for i in range(n):
        pairs += [(2 * i, 2 * (i ^ (1 << bit0))), (2 * i + 1, 2 * (i ^ (1 << bit1)) + 1)]
    return pairs


def my_bit(bit0, bit1):
    index = lax.axis_index("tm")
    return jnp.where(lax.axis_index("rep") == 0, (index >> bit0) & 1, (index >> bit1) & 1)


def sum_over_tm(total):
    order0, order1, rest = bit_orders()
    for bit0, bit1 in zip(order0, order1):
        mine = my_bit(bit0, bit1)
        half = total.shape[0] // 2
        send = lax.dynamic_slice_in_dim(total, (1 - mine) * half, half, 0).astype(BF)
        keep = lax.dynamic_slice_in_dim(total, mine * half, half, 0)
        total = keep + lax.ppermute(send, AXES, partners(bit0, bit1)).astype(F32)
    for bit in rest:
        own = total.astype(BF)
        total = own.astype(F32) + lax.ppermute(own, AXES, partners(bit, bit)).astype(F32)
    whole = total.astype(BF)
    for bit0, bit1 in zip(order0[::-1], order1[::-1]):
        got = lax.ppermute(whole, AXES, partners(bit0, bit1))
        mine = my_bit(bit0, bit1)
        whole = jnp.where(
            mine == 1, jnp.concatenate([got, whole], 0), jnp.concatenate([whole, got], 0)
        )
    return whole


def attend_kernel(decay_ref, q_ref, k_ref, v_ref, g_ref, gap_ref, first_ref, o_ref, dq_ref, dk_ref, dv_ref):
    head = pl.program_id(0)
    rows, keys = q_ref.shape[0], k_ref.shape[0]
    inv_scale = 1.0 / math.sqrt(HD)
    q, k, v, g = q_ref[...], k_ref[...], v_ref[...], g_ref[...]
    at_key = lax.broadcasted_iota(jnp.int32, (rows, keys), 1)
    at_row = lax.broadcasted_iota(jnp.int32, (rows, keys), 0) + (keys - rows)
    allowed = (at_key >= first_ref[...]) & (at_key <= at_row)
    bias = gap_ref[...] * (decay_ref[head] * LOG2E)
    scores = dot(q, k, ((1,), (1,))) * (inv_scale * LOG2E) - bias
    scores = jnp.where(allowed, scores, -1e30)
    weights = jnp.exp2(scores - jnp.max(scores, -1, keepdims=True))
    probs = weights * (1.0 / jnp.sum(weights, -1, keepdims=True))
    low = probs.astype(BF)
    o_ref[...] = dot(low, v).astype(BF)
    dv_ref[...] = dot(low, g, ((0,), (0,))).astype(BF)
    d_probs = dot(g, v, ((1,), (1,)))
    delta = jnp.sum(probs * d_probs, -1, keepdims=True)
    d_scores = (probs * (d_probs - delta)).astype(BF)
    dq_ref[...] = (dot(d_scores, k) * inv_scale).astype(BF)
    dk_ref[...] = (dot(d_scores, q, ((0,), (0,))) * inv_scale).astype(BF)


def attend(q, k, v, g, gap, first, decay):
    rows, width = q.shape
    keys = k.shape[0]
    near = pl.BlockSpec((rows, HD), lambda h: (0, h))
    wide = pl.BlockSpec((keys, HD), lambda h: (0, h))
    return pl.pallas_call(
        attend_kernel,
        grid=(width // HD,),
        in_specs=[
            pl.BlockSpec(memory_space=pltpu.SMEM),
            near,
            wide,
            wide,
            near,
            pl.BlockSpec((1, keys), lambda h: (0, 0)),
            pl.BlockSpec((rows, 1), lambda h: (0, 0)),
        ],
        out_specs=[near, near, wide, wide],
        out_shape=[
            jax.ShapeDtypeStruct((rows, width), BF),
            jax.ShapeDtypeStruct((rows, width), BF),
            jax.ShapeDtypeStruct((keys, width), BF),
            jax.ShapeDtypeStruct((keys, width), BF),
        ],
        compiler_params=pltpu.CompilerParams(vmem_limit_bytes=40 * 1024 * 1024),
        name="attend",
    )(decay, q, k, v, g, gap, first)


def shards(table, cotangent, stamps, starts, w_query, w_key, w_value, w_out, decay):
    n = lax.axis_size("tm")
    index = lax.axis_index("tm")
    core = lax.axis_index("rep")
    blk = table.shape[1]
    width = table.shape[2]
    cols = w_query.shape[1]
    block = jnp.where(core == 0, index, 2 * n - 1 - index)

    x_own = lax.dynamic_index_in_dim(table, core, 0, False)
    g_own = lax.dynamic_index_in_dim(cotangent, core, 0, False)
    t_own = lax.dynamic_index_in_dim(stamps, core, 0, False)
    first = lax.dynamic_index_in_dim(starts, core, 0, False)
    pieces = jnp.stack([t_own & 255, (t_own >> 8) & 255, t_own >> 16]).astype(BF)
    pieces = jnp.pad(pieces, ((0, 13), (0, width - blk)))
    parcel = jnp.concatenate([x_own, pieces], 0)
    back_one = shift_blocks(parcel, 1)
    back_two = shift_blocks(parcel, 2)

    w_all = jnp.concatenate([w_query, w_key, w_value], 1)
    w_all_other = swap_cores(w_all)
    w_out_other = swap_cores(w_out)
    decay_here = jnp.concatenate([decay, swap_cores(decay)])

    def joined(which):
        return jnp.concatenate(
            [w[:, which * cols : (which + 1) * cols] for w in (w_all, w_all_other)], 1
        )

    wq, wk, wv = joined(0), joined(1), joined(2)
    wo = jnp.concatenate([w_out, w_out_other], 0)

    q = dot(x_own, wq).astype(BF)
    g_attn = dot(g_own, wo, ((1,), (1,))).astype(BF)

    x_win = jnp.concatenate([back_two[:blk], back_one[:blk], x_own], 0)

    def times(parcel):
        p = parcel[blk : blk + 3, :blk].astype(F32)
        return p[0] + 256.0 * p[1] + 65536.0 * p[2]

    t_self = t_own.astype(F32)
    t_win = jnp.concatenate([times(back_two), times(back_one), t_self])
    gap = (t_self[-1] - t_win)[None]
    first_local = (first - (block - 2) * blk)[:, None]

    k_win = dot(x_win, wk).astype(BF)
    v_win = dot(x_win, wv).astype(BF)
    attn, dq, dk, dv = attend(q, k_win, v_win, g_attn, gap, first_local, decay_here)

    scale = 1.0 / math.sqrt(2 * blk * n)
    contract = ((0,), (0,))
    term_out = dot(attn, g_own, contract) * scale
    term_value = dot(x_win, dv, contract) * scale
    term_query = dot(x_own, dq, contract) * scale
    term_key = dot(x_win, dk, contract) * scale

    def both_cores(columns, rows=None):
        away = [m[:, cols:] for m in columns]
        here = [m[:, :cols] for m in columns]
        if rows is not None:
            away += [rows[cols:, :cols], rows[cols:, cols:]]
            here += [rows[:cols, :cols], rows[:cols, cols:]]
        return jnp.concatenate(here, 0) + swap_cores(jnp.concatenate(away, 0))

    sum_a = sum_over_tm(both_cores([term_value], term_out))
    sum_b = sum_over_tm(both_cores([term_query, term_key]))

    mixed_own = dot(attn, wo).astype(BF)

    def into_rows(dk_part, dv_part):
        return dot(dk_part, wk, ((1,), (1,))) + dot(dv_part, wv, ((1,), (1,)))

    to_two = into_rows(dk[:blk], dv[:blk]).astype(BF)
    to_one = into_rows(dk[blk : 2 * blk], dv[blk : 2 * blk]).astype(BF)
    to_self = dot(dq, wq, ((1,), (1,))) + into_rows(dk[2 * blk :], dv[2 * blk :])
    grad_own = (
        to_self
        + shift_blocks(to_one, -1).astype(F32)
        + shift_blocks(to_two, -2).astype(F32)
    ).astype(BF)

    def both_blocks(own):
        other = swap_cores(own)
        return jnp.where(core == 0, jnp.stack([own, other]), jnp.stack([other, own]))

    mixed = both_blocks(mixed_own)
    grad_table = both_blocks(grad_own)
    wide = width // 2
    grad_value = sum_a[:width].astype(F32)
    grad_out = jnp.concatenate(
        [sum_a[width : width + cols], sum_a[width + cols :]], 1
    ).astype(F32)
    grad_query = sum_b[:width].astype(F32)
    grad_key = sum_b[width:].astype(F32)
    return (mixed, grad_table, grad_query, grad_key, grad_value, grad_out)


def solution(mesh):
    return jax.shard_map(
        shards,
        mesh=mesh,
        in_specs=(
            P(None, "tm", None),
            P(None, "tm", None),
            P(None, "tm"),
            P(None, "tm"),
            P(None, "rep"),
            P(None, "rep"),
            P(None, "rep"),
            P("rep", None),
            P("rep"),
        ),
        out_specs=(
            P(None, "tm", None),
            P(None, "tm", None),
            P(None, "rep"),
            P(None, "rep"),
            P(None, "rep"),
            P("rep", None),
        ),
        check_vma=False,
    )
```

```python
import functools
import math

import jax
import jax.numpy as jnp
from jax import lax
from jax.experimental import pallas as pl
from jax.experimental.pallas import tpu as pltpu
from jax.sharding import PartitionSpec as P

HD = 128
BF = jnp.bfloat16
F32 = jnp.float32
AXES = ("tm", "rep")
LOG2E = math.log2(math.e)
DOWN = ((0,), (0,))
ACROSS = ((1,), (1,))


def dot(a, b, dims=((1,), (0,))):
    return lax.dot_general(a, b, (dims, ((), ())), preferred_element_type=F32)


def swap_cores(x):
    return lax.ppermute(x, "rep", [(0, 1), (1, 0)])


def shift_blocks(x, distance):
    n = lax.axis_size("tm")

    def worker(b):
        return 2 * b if b < n else 2 * (2 * n - 1 - b) + 1

    route = [(worker(b), worker((b + distance) % (2 * n))) for b in range(2 * n)]
    return lax.ppermute(x, AXES, route)


def bit_orders():
    bits = lax.axis_size("tm").bit_length() - 1
    count = min(3, bits)
    first = list(range(count))
    return first, first[-1:] + first[:-1], list(range(count, bits))


def partners(bit0, bit1):
    n = lax.axis_size("tm")
    pairs = []
    for i in range(n):
        pairs += [(2 * i, 2 * (i ^ (1 << bit0))), (2 * i + 1, 2 * (i ^ (1 << bit1)) + 1)]
    return pairs


def my_bits(orders):
    index = lax.axis_index("tm")
    on_first = lax.axis_index("rep") == 0
    return [jnp.where(on_first, (index >> a) & 1, (index >> b) & 1) for a, b in zip(*orders[:2])]


def tied(x, *others):
    return lax.optimization_barrier((x, *others))[0]


def call(kernel, name, outs, args, smem=1, far_in=0, scratch=(), limit=20, work=1):
    spaces = [pltpu.SMEM] * smem + [pl.ANY] * far_in + [pltpu.VMEM] * (len(args) - smem - far_in)
    return pl.pallas_call(
        kernel,
        in_specs=[pl.BlockSpec(memory_space=space) for space in spaces],
        out_specs=[pl.BlockSpec(memory_space=pltpu.VMEM)] * len(outs),
        out_shape=[jax.ShapeDtypeStruct(shape, dtype) for shape, dtype in outs],
        scratch_shapes=[pltpu.VMEM(shape, dtype) for shape, dtype in scratch]
        + ([pltpu.SemaphoreType.DMA((far_in,))] if far_in else []),
        compiler_params=pltpu.CompilerParams(vmem_limit_bytes=limit << 20),
        cost_estimate=pl.CostEstimate(flops=work << 27, bytes_accessed=work << 17, transcendentals=0),
        name=name,
    )(*args[:smem], *(pltpu.with_memory_space_constraint(x, pltpu.HBM) for x in args[smem : smem + far_in]), *args[smem + far_in :])


CORE, WINDOW, BITS = 0, 1, 2


def places_kernel(info, starts_ref, parcel_ref, first_ref, masks_ref):
    del parcel_ref
    blk = first_ref.shape[0]
    core = info[CORE]
    first = jnp.where(core == 0, starts_ref[0:1], starts_ref[1:2]) - info[WINDOW]
    first_ref[...] = jnp.transpose(jnp.broadcast_to(first, (8, blk)))[:, :1]
    at = lax.broadcasted_iota(jnp.int32, masks_ref.shape, 0)
    masks = jnp.where(at == 0, core, 0)
    for step in range(info.shape[0] - BITS):
        masks = jnp.where(at == step + 1, info[BITS + step], masks)
    masks_ref[...] = masks


def before_kernel(
    info, wq_ref, wk_ref, wv_ref, wo_ref, cotangent_ref, wq_other_ref, wk_other_ref, wv_other_ref, wo_other_ref, x_ref,
    q_ref, k_ref, v_ref, g_attn_ref, g_ref, wq_all_ref, wk_all_ref, wv_all_ref, wo_all_ref, sems,
):
    blk, width = q_ref.shape
    cols = width // 2
    core = info[CORE]
    moves = [
        (wq_ref, wq_all_ref.at[:, :cols]),
        (wk_ref, wk_all_ref.at[:, :cols]),
        (wv_ref, wv_all_ref.at[:, :cols]),
        (wo_ref, wo_all_ref.at[:cols]),
        (cotangent_ref.at[core], g_ref),
    ]
    copies = [pltpu.make_async_copy(a, b, sems.at[i]) for i, (a, b) in enumerate(moves)]
    for copy in copies:
        copy.start()
    wq_all_ref[:, cols:] = wq_other_ref[...]
    wk_all_ref[:, cols:] = wk_other_ref[...]
    wv_all_ref[:, cols:] = wv_other_ref[...]
    wo_all_ref[cols:] = wo_other_ref[...]
    for i, (all_ref, out_ref) in enumerate(((wq_all_ref, q_ref), (wk_all_ref, k_ref), (wv_all_ref, v_ref))):
        copies[i].wait()
        out_ref[...] = dot(x_ref[:blk], all_ref[...]).astype(BF)
    for copy in copies[3:]:
        copy.wait()
    g_attn_ref[...] = dot(g_ref[...], wo_all_ref[...], ACROSS).astype(BF)


def softmax_parts(scores):
    weights = jnp.exp2(scores - jnp.max(scores, -1, keepdims=True))
    return weights * (1.0 / jnp.sum(weights, -1, keepdims=True))


def stamps_of(parcel_ref, blk):
    pieces = parcel_ref[blk:, :blk].astype(F32)
    at = lax.broadcasted_iota(jnp.int32, pieces.shape, 0)
    unit = jnp.where(at == 0, 1.0, jnp.where(at == 1, 256.0, jnp.where(at == 2, 65536.0, 0.0)))
    return jnp.sum(pieces * unit, 0, keepdims=True)


def window_terms(xs, ref, columns, scale):
    blk = ref.shape[0] // len(xs)
    parts = [dot(x[:blk], ref[i * blk : (i + 1) * blk, columns], DOWN) for i, x in enumerate(xs)]
    return functools.reduce(jnp.add, parts) * scale


def forward_kernel(
    scale, decay_ref, decay_other_ref, x_ref, one_ref, two_ref, q_ref, k_ref, v_ref, g_attn_ref, g_ref, wk_ref, wv_ref, first_ref,
    probs_ref, k_win_ref, v_win_ref, away_ref, here_ref, o_ref, dv_ref, shut_ref,
):
    blk, width = q_ref.shape
    cols = width // 2
    k_win_ref[2 * blk :] = k_ref[...]
    v_win_ref[2 * blk :] = v_ref[...]
    at_key = lax.broadcasted_iota(jnp.int32, shut_ref.shape, 1)
    at_row = lax.broadcasted_iota(jnp.int32, shut_ref.shape, 0) + 2 * blk
    allowed = (at_key >= first_ref[...]) & (at_key <= at_row)
    shut_ref[...] = jnp.where(allowed, 0.0, -1e30)
    xs = (two_ref, one_ref, x_ref)
    for i, ref in enumerate(xs[:2]):
        rows = slice(i * blk, (i + 1) * blk)
        k_win_ref[rows] = dot(ref[:blk], wk_ref[...]).astype(BF)
        v_win_ref[rows] = dot(ref[:blk], wv_ref[...]).astype(BF)
    times = [stamps_of(x, blk) for x in xs]
    gap = (times[2][:, blk - 1 :] - jnp.concatenate(times, 1)) * LOG2E
    heads = width // HD
    for head in range(heads):
        c = slice(head * HD, (head + 1) * HD)
        decay = decay_ref[head] if head < heads // 2 else decay_other_ref[head - heads // 2]
        scores = dot(q_ref[:, c], k_win_ref[:, c], ACROSS) * (LOG2E / math.sqrt(HD))
        probs = softmax_parts(scores + (shut_ref[...] - gap * decay))
        probs_ref[head] = probs
        low = probs.astype(BF)
        o_ref[:, c] = dot(low, v_win_ref[:, c]).astype(BF)
        dv_ref[:, c] = dot(low, g_attn_ref[:, c], DOWN).astype(BF)
    for out_ref, lo in ((here_ref, 0), (away_ref, cols)):
        c = slice(lo, lo + cols)
        out_ref[:width] = window_terms(xs, dv_ref, c, scale)
        out_ref[width : width + cols] = dot(o_ref[:, c], g_ref[:, :cols], DOWN) * scale
        out_ref[width + cols :] = dot(o_ref[:, c], g_ref[:, cols:], DOWN) * scale


def backward_kernel(
    scale, x_ref, one_ref, two_ref, q_ref, k_win_ref, v_win_ref, g_attn_ref, probs_ref,
    away_ref, here_ref, dq_ref, dk_ref,
):
    width = q_ref.shape[1]
    cols = width // 2
    inv_scale = 1.0 / math.sqrt(HD)
    for head in range(width // HD):
        c = slice(head * HD, (head + 1) * HD)
        probs = probs_ref[head]
        d_probs = dot(g_attn_ref[:, c], v_win_ref[:, c], ACROSS)
        delta = jnp.sum(probs * d_probs, -1, keepdims=True)
        d_scores = (probs * (d_probs - delta)).astype(BF)
        dq_ref[:, c] = (dot(d_scores, k_win_ref[:, c]) * inv_scale).astype(BF)
        dk_ref[:, c] = (dot(d_scores, q_ref[:, c], DOWN) * inv_scale).astype(BF)
    for out_ref, lo in ((here_ref, 0), (away_ref, cols)):
        c = slice(lo, lo + cols)
        out_ref[:width] = window_terms((x_ref,), dq_ref, c, scale)
        out_ref[width:] = window_terms((two_ref, one_ref, x_ref), dk_ref, c, scale)


def tail_kernel(
    dk_ref, wk_ref, dv_ref, wv_ref, dq_ref, wq_ref, o_ref, wo_ref, two_ref, one_ref, own_ref, mixed_ref
):
    blk = o_ref.shape[0]
    for i, out_ref in enumerate((two_ref, one_ref, own_ref)):
        rows = slice(i * blk, (i + 1) * blk)
        part = dot(dk_ref[rows], wk_ref[...], ACROSS) + dot(dv_ref[rows], wv_ref[...], ACROSS)
        if out_ref is own_ref:
            part += dot(dq_ref[...], wq_ref[...], ACROSS)
        out_ref[...] = part.astype(out_ref.dtype)
    mixed_ref[...] = dot(o_ref[...], wo_ref[...]).astype(BF)


class Summed:
    def __init__(self, masks, orders, here, away):
        self.masks = masks
        self.orders, self.rest = orders[:2], orders[2]
        self.keep, self.got = here, swap_cores(away)

    def passed(self, step, x):
        return lax.ppermute(x, AXES, partners(*(order[step] for order in self.orders)))

    def halve(self, step, *after):
        self.got = tied(self.got, *after)
        half = self.keep.shape[0] // 2
        second = self.masks[step, : self.keep.shape[1]][None] == 1

        def total(rows):
            return self.keep[rows] + self.got[rows].astype(F32)

        lower, upper = total(slice(None, half)), total(slice(half, None))
        self.keep = jnp.where(second, upper, lower)
        self.send = jnp.where(second, lower, upper).astype(BF)
        self.got = self.passed(step, self.send)

    def exchange(self, *after):
        total = self.keep + tied(self.got, *after).astype(F32)
        for bit in self.rest:
            self.send = total.astype(BF)
            got = lax.ppermute(self.send, AXES, partners(bit, bit))
            total = self.send.astype(F32) + got.astype(F32)
        self.whole = total.astype(BF)

    def gather(self, step, *after):
        self.send = self.whole = tied(self.whole, *after)
        self.got = self.passed(step, self.whole)

    def placed(self, step, *after):
        got = tied(self.got, *after)
        second = self.masks[step, : self.keep.shape[1]][None] == 1
        self.parts = jnp.where(second, got, self.whole), jnp.where(second, self.whole, got)
        self.whole = jnp.concatenate(self.parts, 0)


def shards(table, cotangent, stamps, starts, w_query, w_key, w_value, w_out, decay):
    n = lax.axis_size("tm")
    index = lax.axis_index("tm")
    core = lax.axis_index("rep")
    blk = table.shape[1]
    width = table.shape[2]
    cols = w_query.shape[1]
    block = jnp.where(core == 0, index, 2 * n - 1 - index)
    orders = bit_orders()
    info = jnp.stack([core, (block - 2) * blk, *my_bits(orders)]).astype(jnp.int32)

    x_own = lax.dynamic_index_in_dim(table, core, 0, False)
    t_own = lax.dynamic_index_in_dim(stamps, core, 0, False)
    pieces = jnp.stack([t_own & 255, (t_own >> 8) & 255, t_own >> 16]).astype(BF)
    pieces = jnp.pad(pieces, ((0, 13), (0, width - blk)))
    parcel = jnp.concatenate([x_own, pieces], 0)
    back_one = shift_blocks(parcel, 1)
    back_two = shift_blocks(parcel, 2)


    rows = ((blk, width), BF)
    window = ((3 * blk, width), BF)
    square = ((width, width), BF)
    pair = ((2 * width, cols), F32)
    heads = ((width // HD, blk, 3 * blk), F32)
    scale = 1.0 / math.sqrt(2 * blk * n)

    first, masks = call(
        places_kernel, "places", [((blk, 1), jnp.int32), ((8, width), jnp.int32)], (info, starts, parcel), work=0
    )
    others = [swap_cores(tied(x, parcel)) for x in (w_query, w_key, w_value, w_out, decay)]
    decay_other = others.pop()
    q, k_own, v_own, g_attn, g_own, wq, wk, wv, wo = call(
        before_kernel,
        "before",
        [rows, rows, rows, rows, rows, square, square, square, square],
        (info, w_query, w_key, w_value, w_out, cotangent, *others, parcel),
        far_in=5,
        work=0,
    )
    probs, k_win, v_win, away_a, here_a, attn, dv = call(
        functools.partial(forward_kernel, scale),
        "forward",
        [heads, window, window, pair, pair, rows, window],
        (decay, decay_other, parcel, back_one, back_two, q, k_own, v_own, g_attn, g_own, wk, wv, first),
        smem=2,
        scratch=[((blk, 3 * blk), F32)],
        work=32,
    )
    sum_a = Summed(masks[1:], orders, here_a, away_a)
    away_b, here_b, dq, dk = call(
        functools.partial(backward_kernel, scale),
        "backward",
        [pair, pair, rows, window],
        (parcel, back_one, back_two, q, k_win, v_win, g_attn, probs),
        smem=0,
        work=24,
    )
    sum_b = Summed(masks[1:], orders, here_b, away_b)
    to_two, to_one, to_self, mixed_own = call(
        tail_kernel, "tail", [rows, rows, ((blk, width), F32), rows], (dk, wk, dv, wv, dq, wq, attn, wo), smem=0, work=8
    )
    steps = len(orders[0])
    halos = []

    def start_halos(*after):
        halos.append(shift_blocks(tied(to_one, *after), -1))
        halos.append(shift_blocks(tied(to_two, *after), -2))

    def end_halos():
        return (to_self + halos[0].astype(F32) + halos[1].astype(F32)).astype(BF)

    sum_a.halve(0)
    sum_b.halve(0, sum_a.send)
    sum_a.halve(1, sum_b.send)
    sum_b.halve(1, sum_a.send)
    sum_a.halve(2, sum_b.send)
    sum_b.halve(2, sum_a.send)
    start_halos(sum_b.send)
    sum_a.exchange(sum_b.send)
    sum_b.exchange(sum_a.send)
    sum_a.gather(2, sum_b.send)
    sum_b.gather(2, sum_a.send)
    sum_a.placed(2)
    sum_b.placed(2, sum_a.whole)
    sum_a.gather(1, sum_b.send)
    sum_b.gather(1, sum_a.send)
    sum_a.placed(1)
    sum_b.placed(1, sum_a.whole)
    sum_a.gather(0, sum_b.send)
    sum_b.gather(0, sum_a.send)
    sum_a.placed(0)
    grad_own = end_halos()
    on_second = masks[0][None, None] == 1

    def both_blocks(own):
        other = swap_cores(own)
        return jnp.where(on_second, jnp.stack([other, own]), jnp.stack([own, other]))

    mixed = both_blocks(mixed_own)
    grad_table = both_blocks(grad_own)
    grad_value, lines = (part.astype(F32) for part in sum_a.parts)
    grad_out = jnp.concatenate([lines[:cols], lines[cols:]], 1)
    sum_b.placed(0, grad_value, grad_out)
    grad_query, grad_key = (part.astype(F32) for part in sum_b.parts)
    return (mixed, grad_table, grad_query, grad_key, grad_value, grad_out)


def solution(mesh):
    return jax.shard_map(
        shards,
        mesh=mesh,
        in_specs=(
            P(None, "tm", None),
            P(None, "tm", None),
            P(None, "tm"),
            P(None, "tm"),
            P(None, "rep"),
            P(None, "rep"),
            P(None, "rep"),
            P("rep", None),
            P("rep"),
        ),
        out_specs=(
            P(None, "tm", None),
            P(None, "tm", None),
            P(None, "rep"),
            P(None, "rep"),
            P(None, "rep"),
            P("rep", None),
        ),
        check_vma=False,
    )
```

```python
import functools
import math

import jax
import jax.numpy as jnp
from jax import lax
from jax.experimental import pallas as pl
from jax.experimental.pallas import tpu as pltpu
from jax.sharding import PartitionSpec as P

HD = 128
BF = jnp.bfloat16
F32 = jnp.float32
AXES = ("tm", "rep")
LOG2E = math.log2(math.e)
DOWN = ((0,), (0,))
ACROSS = ((1,), (1,))


def dot(a, b, dims=((1,), (0,))):
    return lax.dot_general(a, b, (dims, ((), ())), preferred_element_type=F32)


def swap_cores(x):
    return lax.ppermute(x, "rep", [(0, 1), (1, 0)])


def shift_blocks(x, distance):
    n = lax.axis_size("tm")

    def worker(b):
        return 2 * b if b < n else 2 * (2 * n - 1 - b) + 1

    route = [(worker(b), worker((b + distance) % (2 * n))) for b in range(2 * n)]
    return lax.ppermute(x, AXES, route)


def bit_orders():
    bits = lax.axis_size("tm").bit_length() - 1
    count = min(3, bits)
    first = list(range(count))
    return first[-1:] + first[:-1], first, list(range(count, bits))


def partners(bit0, bit1):
    n = lax.axis_size("tm")
    pairs = []
    for i in range(n):
        pairs += [(2 * i, 2 * (i ^ (1 << bit0))), (2 * i + 1, 2 * (i ^ (1 << bit1)) + 1)]
    return pairs


def my_bits(orders):
    index = lax.axis_index("tm")
    on_first = lax.axis_index("rep") == 0
    return [jnp.where(on_first, (index >> a) & 1, (index >> b) & 1) for a, b in zip(*orders[:2])]


def tied(x, *others):
    return lax.optimization_barrier((x, *others))[0]


def call(kernel, name, outs, args, smem=1, far_in=0, scratch=(), limit=20, work=1):
    spaces = [pltpu.SMEM] * smem + [pl.ANY] * far_in + [pltpu.VMEM] * (len(args) - smem - far_in)
    return pl.pallas_call(
        kernel,
        in_specs=[pl.BlockSpec(memory_space=space) for space in spaces],
        out_specs=[pl.BlockSpec(memory_space=pltpu.VMEM)] * len(outs),
        out_shape=[jax.ShapeDtypeStruct(shape, dtype) for shape, dtype in outs],
        scratch_shapes=[pltpu.VMEM(shape, dtype) for shape, dtype in scratch]
        + ([pltpu.SemaphoreType.DMA((far_in,))] if far_in else []),
        compiler_params=pltpu.CompilerParams(vmem_limit_bytes=limit << 20),
        cost_estimate=pl.CostEstimate(flops=work << 27, bytes_accessed=work << 17, transcendentals=0),
        name=name,
    )(*args[:smem], *(pltpu.with_memory_space_constraint(x, pltpu.HBM) for x in args[smem : smem + far_in]), *args[smem + far_in :])


CORE, WINDOW, BITS = 0, 1, 2


def places_kernel(info, starts_ref, parcel_ref, shut_ref, masks_ref):
    del parcel_ref
    blk, keys = shut_ref.shape
    core = info[CORE]
    first = jnp.where(core == 0, starts_ref[0:1], starts_ref[1:2]) - info[WINDOW]
    first = jnp.transpose(jnp.broadcast_to(first, (8, blk)))[:, :1]
    at_key = lax.broadcasted_iota(jnp.int32, (blk, keys), 1)
    at_row = lax.broadcasted_iota(jnp.int32, (blk, keys), 0) + (keys - blk)
    shut_ref[...] = jnp.where((at_key >= first) & (at_key <= at_row), 0.0, -1e30)
    at = lax.broadcasted_iota(jnp.int32, masks_ref.shape, 0)
    masks = jnp.where(at == 0, core, 0)
    for step in range(info.shape[0] - BITS):
        masks = jnp.where(at == step + 1, info[BITS + step], masks)
    masks_ref[...] = masks


def before_kernel(
    info, wq_ref, wk_ref, wv_ref, wo_ref, cotangent_ref, wq_other_ref, wk_other_ref, wv_other_ref, wo_other_ref, x_ref,
    q_ref, k_ref, v_ref, g_attn_ref, g_ref, wq_all_ref, wk_all_ref, wv_all_ref, wo_all_ref, sems,
):
    blk, width = q_ref.shape
    cols = width // 2
    core = info[CORE]
    moves = [
        (wq_ref, wq_all_ref.at[:, :cols]),
        (wk_ref, wk_all_ref.at[:, :cols]),
        (wv_ref, wv_all_ref.at[:, :cols]),
        (wo_ref, wo_all_ref.at[:cols]),
        (cotangent_ref.at[core], g_ref),
    ]
    copies = [pltpu.make_async_copy(a, b, sems.at[i]) for i, (a, b) in enumerate(moves)]
    for copy in copies:
        copy.start()
    wq_all_ref[:, cols:] = wq_other_ref[...]
    wk_all_ref[:, cols:] = wk_other_ref[...]
    wv_all_ref[:, cols:] = wv_other_ref[...]
    wo_all_ref[cols:] = wo_other_ref[...]
    for i, (all_ref, out_ref) in enumerate(((wq_all_ref, q_ref), (wk_all_ref, k_ref), (wv_all_ref, v_ref))):
        copies[i].wait()
        out_ref[...] = dot(x_ref[:blk], all_ref[...]).astype(BF)
    for copy in copies[3:]:
        copy.wait()
    g_attn_ref[...] = dot(g_ref[...], wo_all_ref[...], ACROSS).astype(BF)


def softmax_parts(scores):
    weights = jnp.exp2(scores - jnp.max(scores, -1, keepdims=True))
    return weights * (1.0 / jnp.sum(weights, -1, keepdims=True))


def stamps_of(parcel_ref, blk):
    pieces = parcel_ref[blk:, :blk].astype(F32)
    at = lax.broadcasted_iota(jnp.int32, pieces.shape, 0)
    unit = jnp.where(at == 0, 1.0, jnp.where(at == 1, 256.0, jnp.where(at == 2, 65536.0, 0.0)))
    return jnp.sum(pieces * unit, 0, keepdims=True)


def window_terms(xs, ref, columns, scale):
    blk = ref.shape[0] // len(xs)
    parts = [dot(x[:blk], ref[i * blk : (i + 1) * blk, columns], DOWN) for i, x in enumerate(xs)]
    return functools.reduce(jnp.add, parts) * scale


def forward_kernel(
    scale, decay_ref, decay_other_ref, x_ref, one_ref, two_ref, q_ref, k_ref, v_ref, g_attn_ref, g_ref, wk_ref, wv_ref, shut_ref,
    probs_ref, k_win_ref, v_win_ref, away_ref, here_ref, o_ref, dv_ref,
):
    blk, width = q_ref.shape
    cols = width // 2
    k_win_ref[2 * blk :] = k_ref[...]
    v_win_ref[2 * blk :] = v_ref[...]
    xs = (two_ref, one_ref, x_ref)
    for i, ref in enumerate(xs[:2]):
        rows = slice(i * blk, (i + 1) * blk)
        k_win_ref[rows] = dot(ref[:blk], wk_ref[...]).astype(BF)
        v_win_ref[rows] = dot(ref[:blk], wv_ref[...]).astype(BF)
    times = [stamps_of(x, blk) for x in xs]
    gap = (times[2][:, blk - 1 :] - jnp.concatenate(times, 1)) * LOG2E
    heads = width // HD
    lanes = [slice(head * HD, (head + 1) * HD) for head in range(heads)]

    def scores_of(head):
        c = lanes[head]
        return dot(q_ref[:, c], k_win_ref[:, c], ACROSS)

    ahead = scores_of(0)
    low = None
    for head in range(heads + 1):
        scores = ahead
        if head + 1 < heads:
            ahead = scores_of(head + 1)
        before = low
        if head < heads:
            decay = decay_ref[head] if head < heads // 2 else decay_other_ref[head - heads // 2]
            probs = softmax_parts(scores * (LOG2E / math.sqrt(HD)) + (shut_ref[...] - gap * decay))
            probs_ref[head] = probs
            low = probs.astype(BF)
        if head:
            c = lanes[head - 1]
            o_ref[:, c] = dot(before, v_win_ref[:, c]).astype(BF)
            dv_ref[:, c] = dot(before, g_attn_ref[:, c], DOWN).astype(BF)
    for out_ref, lo in ((here_ref, 0), (away_ref, cols)):
        c = slice(lo, lo + cols)
        out_ref[:width] = window_terms(xs, dv_ref, c, scale)
        out_ref[width : width + cols] = dot(o_ref[:, c], g_ref[:, :cols], DOWN) * scale
        out_ref[width + cols :] = dot(o_ref[:, c], g_ref[:, cols:], DOWN) * scale


def backward_kernel(
    scale, x_ref, one_ref, two_ref, q_ref, k_win_ref, v_win_ref, g_attn_ref, probs_ref,
    away_ref, here_ref, dq_ref, dk_ref,
):
    width = q_ref.shape[1]
    cols = width // 2
    inv_scale = 1.0 / math.sqrt(HD)
    heads = width // HD
    lanes = [slice(head * HD, (head + 1) * HD) for head in range(heads)]

    def d_probs_of(head):
        return dot(g_attn_ref[:, lanes[head]], v_win_ref[:, lanes[head]], ACROSS)

    ahead = d_probs_of(0)
    d_scores = None
    for head in range(heads + 1):
        d_probs = ahead
        if head + 1 < heads:
            ahead = d_probs_of(head + 1)
        if head:
            c = lanes[head - 1]
            dq_ref[:, c] = (dot(d_scores, k_win_ref[:, c]) * inv_scale).astype(BF)
            dk_ref[:, c] = (dot(d_scores, q_ref[:, c], DOWN) * inv_scale).astype(BF)
        if head < heads:
            probs = probs_ref[head]
            delta = jnp.sum(probs * d_probs, -1, keepdims=True)
            d_scores = (probs * (d_probs - delta)).astype(BF)
    for out_ref, lo in ((here_ref, 0), (away_ref, cols)):
        c = slice(lo, lo + cols)
        out_ref[:width] = window_terms((x_ref,), dq_ref, c, scale)
        out_ref[width:] = window_terms((two_ref, one_ref, x_ref), dk_ref, c, scale)


def tail_kernel(
    dk_ref, wk_ref, dv_ref, wv_ref, dq_ref, wq_ref, o_ref, wo_ref, two_ref, one_ref, own_ref, mixed_ref
):
    blk = o_ref.shape[0]
    for i, out_ref in enumerate((two_ref, one_ref, own_ref)):
        rows = slice(i * blk, (i + 1) * blk)
        part = dot(dk_ref[rows], wk_ref[...], ACROSS) + dot(dv_ref[rows], wv_ref[...], ACROSS)
        if out_ref is own_ref:
            part += dot(dq_ref[...], wq_ref[...], ACROSS)
        out_ref[...] = part.astype(out_ref.dtype)
    mixed_ref[...] = dot(o_ref[...], wo_ref[...]).astype(BF)


class Summed:
    def __init__(self, masks, orders, here, away):
        self.masks = masks
        self.orders, self.rest = orders[:2], orders[2]
        self.keep, self.got = here, swap_cores(away)

    def passed(self, step, x):
        return lax.ppermute(x, AXES, partners(*(order[step] for order in self.orders)))

    def halve(self, step, *after):
        self.got = tied(self.got, *after)
        half = self.keep.shape[0] // 2
        second = self.masks[step, : self.keep.shape[1]][None] == 1

        def total(rows):
            return self.keep[rows] + self.got[rows].astype(F32)

        lower, upper = total(slice(None, half)), total(slice(half, None))
        self.keep = jnp.where(second, upper, lower)
        self.send = jnp.where(second, lower, upper).astype(BF)
        self.got = self.passed(step, self.send)

    def exchange(self, *after):
        total = self.keep + tied(self.got, *after).astype(F32)
        for bit in self.rest:
            self.send = total.astype(BF)
            got = lax.ppermute(self.send, AXES, partners(bit, bit))
            total = self.send.astype(F32) + got.astype(F32)
        self.whole = total.astype(BF)

    def gather(self, step, *after):
        self.send = self.whole = tied(self.whole, *after)
        self.got = self.passed(step, self.whole)

    def placed(self, step, *after):
        got = tied(self.got, *after)
        second = self.masks[step, : self.keep.shape[1]][None] == 1
        self.parts = jnp.where(second, got, self.whole), jnp.where(second, self.whole, got)
        self.whole = jnp.concatenate(self.parts, 0)


def shards(table, cotangent, stamps, starts, w_query, w_key, w_value, w_out, decay):
    n = lax.axis_size("tm")
    index = lax.axis_index("tm")
    core = lax.axis_index("rep")
    blk = table.shape[1]
    width = table.shape[2]
    cols = w_query.shape[1]
    block = jnp.where(core == 0, index, 2 * n - 1 - index)
    orders = bit_orders()
    info = jnp.stack([core, (block - 2) * blk, *my_bits(orders)]).astype(jnp.int32)

    x_own = lax.dynamic_index_in_dim(table, core, 0, False)
    t_own = lax.dynamic_index_in_dim(stamps, core, 0, False)
    pieces = jnp.stack([t_own & 255, (t_own >> 8) & 255, t_own >> 16]).astype(BF)
    pieces = jnp.pad(pieces, ((0, 13), (0, width - blk)))
    parcel = jnp.concatenate([x_own, pieces], 0)
    back_one = shift_blocks(parcel, 1)
    back_two = shift_blocks(parcel, 2)


    rows = ((blk, width), BF)
    window = ((3 * blk, width), BF)
    square = ((width, width), BF)
    pair = ((2 * width, cols), F32)
    heads = ((width // HD, blk, 3 * blk), F32)
    scale = 1.0 / math.sqrt(2 * blk * n)

    shut, masks = call(
        places_kernel, "places", [((blk, 3 * blk), F32), ((8, width), jnp.int32)], (info, starts, parcel), work=0
    )
    others = [swap_cores(tied(x, parcel)) for x in (w_query, w_key, w_value, w_out, decay)]
    decay_other = others.pop()
    q, k_own, v_own, g_attn, g_own, wq, wk, wv, wo = call(
        before_kernel,
        "before",
        [rows, rows, rows, rows, rows, square, square, square, square],
        (info, w_query, w_key, w_value, w_out, cotangent, *others, parcel),
        far_in=5,
        work=0,
    )
    probs, k_win, v_win, away_a, here_a, attn, dv = call(
        functools.partial(forward_kernel, scale),
        "forward",
        [heads, window, window, pair, pair, rows, window],
        (decay, decay_other, parcel, back_one, back_two, q, k_own, v_own, g_attn, g_own, wk, wv, shut),
        smem=2,
        work=32,
    )
    sum_a = Summed(masks[1:], orders, here_a, away_a)
    away_b, here_b, dq, dk = call(
        functools.partial(backward_kernel, scale),
        "backward",
        [pair, pair, rows, window],
        (parcel, back_one, back_two, q, k_win, v_win, g_attn, probs),
        smem=0,
        work=24,
    )
    sum_b = Summed(masks[1:], orders, here_b, away_b)
    to_two, to_one, to_self, mixed_own = call(
        tail_kernel, "tail", [rows, rows, ((blk, width), F32), rows], (dk, wk, dv, wv, dq, wq, attn, wo), smem=0, work=8
    )
    steps = len(orders[0])
    for step in range(steps):
        sum_a.halve(step, *([sum_b.send] if step else []))
        sum_b.halve(step, sum_a.send)
    halo_one = shift_blocks(tied(to_one, sum_b.send), -1)
    halo_two = shift_blocks(tied(to_two, sum_b.send), -2)
    sum_a.exchange(sum_b.send)
    sum_b.exchange(sum_a.send)
    for step in reversed(range(steps)):
        sum_a.gather(step, sum_b.send)
        sum_b.gather(step, sum_a.send)
        sum_a.placed(step)
        if step:
            sum_b.placed(step, sum_a.whole)
    grad_own = (to_self + halo_one.astype(F32) + halo_two.astype(F32)).astype(BF)
    on_second = masks[0][None, None] == 1

    def both_blocks(own):
        other = swap_cores(own)
        return jnp.where(on_second, jnp.stack([other, own]), jnp.stack([own, other]))

    mixed = both_blocks(mixed_own)
    grad_table = both_blocks(grad_own)
    grad_value, lines = (part.astype(F32) for part in sum_a.parts)
    grad_out = jnp.concatenate([lines[:cols], lines[cols:]], 1)
    sum_b.placed(0, grad_value, grad_out)
    grad_query, grad_key = (part.astype(F32) for part in sum_b.parts)
    return (mixed, grad_table, grad_query, grad_key, grad_value, grad_out)


def solution(mesh):
    return jax.shard_map(
        shards,
        mesh=mesh,
        in_specs=(
            P(None, "tm", None),
            P(None, "tm", None),
            P(None, "tm"),
            P(None, "tm"),
            P(None, "rep"),
            P(None, "rep"),
            P(None, "rep"),
            P("rep", None),
            P("rep"),
        ),
        out_specs=(
            P(None, "tm", None),
            P(None, "tm", None),
            P(None, "rep"),
            P(None, "rep"),
            P(None, "rep"),
            P("rep", None),
        ),
        check_vma=False,
    )
```

```python
import functools
import math

import jax
import jax.numpy as jnp
from jax import lax
from jax.experimental import pallas as pl
from jax.experimental.pallas import tpu as pltpu
from jax.sharding import PartitionSpec as P

HD = 128
BF = jnp.bfloat16
F32 = jnp.float32
AXES = ("tm", "rep")
LOG2E = math.log2(math.e)
DOWN = ((0,), (0,))
ACROSS = ((1,), (1,))


def dot(a, b, dims=((1,), (0,))):
    return lax.dot_general(a, b, (dims, ((), ())), preferred_element_type=F32)


def swap_cores(x):
    return lax.ppermute(x, "rep", [(0, 1), (1, 0)])


def shift_blocks(x, distance):
    n = lax.axis_size("tm")

    def worker(b):
        return 2 * b if b < n else 2 * (2 * n - 1 - b) + 1

    route = [(worker(b), worker((b + distance) % (2 * n))) for b in range(2 * n)]
    return lax.ppermute(x, AXES, route)


def bit_orders():
    bits = lax.axis_size("tm").bit_length() - 1
    count = min(3, bits)
    first = list(range(count))
    return first[1:] + first[:1], first, list(range(count, bits))


def partners(bit0, bit1):
    n = lax.axis_size("tm")
    pairs = []
    for i in range(n):
        pairs += [(2 * i, 2 * (i ^ (1 << bit0))), (2 * i + 1, 2 * (i ^ (1 << bit1)) + 1)]
    return pairs


def my_bits(orders):
    index = lax.axis_index("tm")
    on_first = lax.axis_index("rep") == 0
    return [jnp.where(on_first, (index >> a) & 1, (index >> b) & 1) for a, b in zip(*orders[:2])]


def tied(x, *others):
    return lax.optimization_barrier((x, *others))[0]


def call(kernel, name, outs, args, smem=1, far_in=0, scratch=(), limit=20, work=1):
    spaces = [pltpu.SMEM] * smem + [pl.ANY] * far_in + [pltpu.VMEM] * (len(args) - smem - far_in)
    return pl.pallas_call(
        kernel,
        in_specs=[pl.BlockSpec(memory_space=space) for space in spaces],
        out_specs=[pl.BlockSpec(memory_space=pltpu.VMEM)] * len(outs),
        out_shape=[jax.ShapeDtypeStruct(shape, dtype) for shape, dtype in outs],
        scratch_shapes=[pltpu.VMEM(shape, dtype) for shape, dtype in scratch]
        + ([pltpu.SemaphoreType.DMA((far_in,))] if far_in else []),
        compiler_params=pltpu.CompilerParams(vmem_limit_bytes=limit << 20),
        cost_estimate=pl.CostEstimate(flops=work << 27, bytes_accessed=work << 17, transcendentals=0),
        name=name,
    )(*args[:smem], *(pltpu.with_memory_space_constraint(x, pltpu.HBM) for x in args[smem : smem + far_in]), *args[smem + far_in :])


CORE, WINDOW, BITS = 0, 1, 2


def places_kernel(info, starts_ref, parcel_ref, shut_ref, masks_ref):
    del parcel_ref
    blk, keys = shut_ref.shape
    core = info[CORE]
    first = jnp.where(core == 0, starts_ref[0:1], starts_ref[1:2]) - info[WINDOW]
    first = jnp.transpose(jnp.broadcast_to(first, (8, blk)))[:, :1]
    at_key = lax.broadcasted_iota(jnp.int32, (blk, keys), 1)
    at_row = lax.broadcasted_iota(jnp.int32, (blk, keys), 0) + (keys - blk)
    shut_ref[...] = jnp.where((at_key >= first) & (at_key <= at_row), 0.0, -1e30)
    at = lax.broadcasted_iota(jnp.int32, masks_ref.shape, 0)
    masks = jnp.where(at == 0, core, 0)
    for step in range(info.shape[0] - BITS):
        masks = jnp.where(at == step + 1, info[BITS + step], masks)
    masks_ref[...] = masks


def before_kernel(
    info, wq_ref, wk_ref, wv_ref, wo_ref, cotangent_ref, wq_other_ref, wk_other_ref, wv_other_ref, wo_other_ref, x_ref,
    q_ref, k_ref, v_ref, g_attn_ref, g_ref, wq_all_ref, wk_all_ref, wv_all_ref, wo_all_ref, sems,
):
    blk, width = q_ref.shape
    cols = width // 2
    core = info[CORE]
    moves = [
        (wq_ref, wq_all_ref.at[:, :cols]),
        (wk_ref, wk_all_ref.at[:, :cols]),
        (wv_ref, wv_all_ref.at[:, :cols]),
        (wo_ref, wo_all_ref.at[:cols]),
        (cotangent_ref.at[core], g_ref),
    ]
    copies = [pltpu.make_async_copy(a, b, sems.at[i]) for i, (a, b) in enumerate(moves)]
    for copy in copies:
        copy.start()
    wq_all_ref[:, cols:] = wq_other_ref[...]
    wk_all_ref[:, cols:] = wk_other_ref[...]
    wv_all_ref[:, cols:] = wv_other_ref[...]
    wo_all_ref[cols:] = wo_other_ref[...]
    for i, (all_ref, out_ref) in enumerate(((wq_all_ref, q_ref), (wk_all_ref, k_ref), (wv_all_ref, v_ref))):
        copies[i].wait()
        out_ref[...] = dot(x_ref[:blk], all_ref[...]).astype(BF)
    for copy in copies[3:]:
        copy.wait()
    g_attn_ref[...] = dot(g_ref[...], wo_all_ref[...], ACROSS).astype(BF)


def softmax_parts(scores):
    weights = jnp.exp2(scores - jnp.max(scores, -1, keepdims=True))
    return weights * (1.0 / jnp.sum(weights, -1, keepdims=True))


def stamps_of(parcel_ref, blk):
    pieces = parcel_ref[blk:, :blk].astype(F32)
    at = lax.broadcasted_iota(jnp.int32, pieces.shape, 0)
    unit = jnp.where(at == 0, 1.0, jnp.where(at == 1, 256.0, jnp.where(at == 2, 65536.0, 0.0)))
    return jnp.sum(pieces * unit, 0, keepdims=True)


def window_terms(xs, ref, columns, scale):
    blk = ref.shape[0] // len(xs)
    parts = [dot(x[:blk], ref[i * blk : (i + 1) * blk, columns], DOWN) for i, x in enumerate(xs)]
    return functools.reduce(jnp.add, parts) * scale


def forward_kernel(
    scale, decay_ref, decay_other_ref, x_ref, one_ref, two_ref, q_ref, k_ref, v_ref, g_attn_ref, g_ref, wk_ref, wv_ref, shut_ref,
    probs_ref, k_win_ref, v_win_ref, away_ref, here_ref, o_ref, dv_ref,
):
    blk, width = q_ref.shape
    cols = width // 2
    k_win_ref[2 * blk :] = k_ref[...]
    v_win_ref[2 * blk :] = v_ref[...]
    xs = (two_ref, one_ref, x_ref)
    for i, ref in enumerate(xs[:2]):
        rows = slice(i * blk, (i + 1) * blk)
        k_win_ref[rows] = dot(ref[:blk], wk_ref[...]).astype(BF)
        v_win_ref[rows] = dot(ref[:blk], wv_ref[...]).astype(BF)
    times = [stamps_of(x, blk) for x in xs]
    gap = (times[2][:, blk - 1 :] - jnp.concatenate(times, 1)) * LOG2E
    heads = width // HD
    lanes = [slice(head * HD, (head + 1) * HD) for head in range(heads)]

    def scores_of(head):
        c = lanes[head]
        return dot(q_ref[:, c], k_win_ref[:, c], ACROSS)

    ahead = scores_of(0)
    low = None
    for head in range(heads + 1):
        scores = ahead
        if head + 1 < heads:
            ahead = scores_of(head + 1)
        before = low
        if head < heads:
            decay = decay_ref[head] if head < heads // 2 else decay_other_ref[head - heads // 2]
            probs = softmax_parts(scores * (LOG2E / math.sqrt(HD)) + (shut_ref[...] - gap * decay))
            probs_ref[head] = probs
            low = probs.astype(BF)
        if head:
            c = lanes[head - 1]
            o_ref[:, c] = dot(before, v_win_ref[:, c]).astype(BF)
            dv_ref[:, c] = dot(before, g_attn_ref[:, c], DOWN).astype(BF)
    for out_ref, lo in ((here_ref, 0), (away_ref, cols)):
        c = slice(lo, lo + cols)
        out_ref[:width] = window_terms(xs, dv_ref, c, scale)
        out_ref[width : width + cols] = dot(o_ref[:, c], g_ref[:, :cols], DOWN) * scale
        out_ref[width + cols :] = dot(o_ref[:, c], g_ref[:, cols:], DOWN) * scale


def backward_kernel(
    scale, x_ref, one_ref, two_ref, q_ref, k_win_ref, v_win_ref, g_attn_ref, probs_ref,
    away_ref, here_ref, dq_ref, dk_ref,
):
    width = q_ref.shape[1]
    cols = width // 2
    inv_scale = 1.0 / math.sqrt(HD)
    heads = width // HD
    lanes = [slice(head * HD, (head + 1) * HD) for head in range(heads)]

    def d_probs_of(head):
        return dot(g_attn_ref[:, lanes[head]], v_win_ref[:, lanes[head]], ACROSS)

    ahead = d_probs_of(0)
    d_scores = None
    for head in range(heads + 1):
        d_probs = ahead
        if head + 1 < heads:
            ahead = d_probs_of(head + 1)
        if head:
            c = lanes[head - 1]
            dq_ref[:, c] = (dot(d_scores, k_win_ref[:, c]) * inv_scale).astype(BF)
            dk_ref[:, c] = (dot(d_scores, q_ref[:, c], DOWN) * inv_scale).astype(BF)
        if head < heads:
            probs = probs_ref[head]
            delta = jnp.sum(probs * d_probs, -1, keepdims=True)
            d_scores = (probs * (d_probs - delta)).astype(BF)
    for out_ref, lo in ((here_ref, 0), (away_ref, cols)):
        c = slice(lo, lo + cols)
        out_ref[:width] = window_terms((x_ref,), dq_ref, c, scale)
        out_ref[width:] = window_terms((two_ref, one_ref, x_ref), dk_ref, c, scale)


def tail_kernel(
    dk_ref, wk_ref, dv_ref, wv_ref, dq_ref, wq_ref, o_ref, wo_ref, two_ref, one_ref, own_ref, mixed_ref
):
    blk = o_ref.shape[0]
    for i, out_ref in enumerate((two_ref, one_ref, own_ref)):
        rows = slice(i * blk, (i + 1) * blk)
        part = dot(dk_ref[rows], wk_ref[...], ACROSS) + dot(dv_ref[rows], wv_ref[...], ACROSS)
        if out_ref is own_ref:
            part += dot(dq_ref[...], wq_ref[...], ACROSS)
        out_ref[...] = part.astype(out_ref.dtype)
    mixed_ref[...] = dot(o_ref[...], wo_ref[...]).astype(BF)


class Summed:
    def __init__(self, masks, orders, here, away):
        self.masks = masks
        self.orders, self.rest = orders[:2], orders[2]
        self.keep, self.got = here, swap_cores(away)

    def passed(self, step, x):
        return lax.ppermute(x, AXES, partners(*(order[step] for order in self.orders)))

    def halve(self, step, *after):
        self.got = tied(self.got, *after)
        half = self.keep.shape[0] // 2
        second = self.masks[step, : self.keep.shape[1]][None] == 1

        def total(rows):
            return self.keep[rows] + self.got[rows].astype(F32)

        lower, upper = total(slice(None, half)), total(slice(half, None))
        self.keep = jnp.where(second, upper, lower)
        self.send = jnp.where(second, lower, upper).astype(BF)
        self.got = self.passed(step, self.send)

    def exchange(self, *after):
        total = self.keep + tied(self.got, *after).astype(F32)
        for bit in self.rest:
            self.send = total.astype(BF)
            got = lax.ppermute(self.send, AXES, partners(bit, bit))
            total = self.send.astype(F32) + got.astype(F32)
        self.whole = total.astype(BF)

    def gather(self, step, *after):
        self.send = self.whole = tied(self.whole, *after)
        self.got = self.passed(step, self.whole)

    def placed(self, step, *after):
        got = tied(self.got, *after)
        second = self.masks[step, : self.keep.shape[1]][None] == 1
        self.parts = jnp.where(second, got, self.whole), jnp.where(second, self.whole, got)
        self.whole = jnp.concatenate(self.parts, 0)


def shards(table, cotangent, stamps, starts, w_query, w_key, w_value, w_out, decay):
    n = lax.axis_size("tm")
    index = lax.axis_index("tm")
    core = lax.axis_index("rep")
    blk = table.shape[1]
    width = table.shape[2]
    cols = w_query.shape[1]
    block = jnp.where(core == 0, index, 2 * n - 1 - index)
    orders = bit_orders()
    info = jnp.stack([core, (block - 2) * blk, *my_bits(orders)]).astype(jnp.int32)

    x_own = lax.dynamic_index_in_dim(table, core, 0, False)
    t_own = lax.dynamic_index_in_dim(stamps, core, 0, False)
    pieces = jnp.stack([t_own & 255, (t_own >> 8) & 255, t_own >> 16]).astype(BF)
    pieces = jnp.pad(pieces, ((0, 13), (0, width - blk)))
    parcel = jnp.concatenate([x_own, pieces], 0)
    back_one = shift_blocks(parcel, 1)
    back_two = shift_blocks(parcel, 2)


    rows = ((blk, width), BF)
    window = ((3 * blk, width), BF)
    square = ((width, width), BF)
    pair = ((2 * width, cols), F32)
    heads = ((width // HD, blk, 3 * blk), F32)
    scale = 1.0 / math.sqrt(2 * blk * n)

    shut, masks = call(
        places_kernel, "places", [((blk, 3 * blk), F32), ((8, width), jnp.int32)], (info, starts, parcel), work=0
    )
    others = [swap_cores(tied(x, parcel)) for x in (w_query, w_key, w_value, w_out, decay)]
    decay_other = others.pop()
    q, k_own, v_own, g_attn, g_own, wq, wk, wv, wo = call(
        before_kernel,
        "before",
        [rows, rows, rows, rows, rows, square, square, square, square],
        (info, w_query, w_key, w_value, w_out, cotangent, *others, parcel),
        far_in=5,
        work=0,
    )
    probs, k_win, v_win, away_a, here_a, attn, dv = call(
        functools.partial(forward_kernel, scale),
        "forward",
        [heads, window, window, pair, pair, rows, window],
        (decay, decay_other, parcel, back_one, back_two, q, k_own, v_own, g_attn, g_own, wk, wv, shut),
        smem=2,
        work=32,
    )
    sum_a = Summed(masks[1:], orders, here_a, away_a)
    away_b, here_b, dq, dk = call(
        functools.partial(backward_kernel, scale),
        "backward",
        [pair, pair, rows, window],
        (parcel, back_one, back_two, q, k_win, v_win, g_attn, probs),
        smem=0,
        work=24,
    )
    sum_b = Summed(masks[1:], orders, here_b, away_b)
    to_two, to_one, to_self, mixed_own = call(
        tail_kernel, "tail", [rows, rows, ((blk, width), F32), rows], (dk, wk, dv, wv, dq, wq, attn, wo), smem=0, work=8
    )
    steps = len(orders[0])
    for step in range(steps):
        sum_a.halve(step, *([sum_b.send] if step else []))
        sum_b.halve(step, sum_a.send)
        if step == min(1, steps - 1):
            halo_one = shift_blocks(tied(to_one, sum_b.send), -1)
        if step == steps - 1:
            halo_two = shift_blocks(tied(to_two, sum_b.send), -2)
    sum_a.exchange(sum_b.send)
    sum_b.exchange(sum_a.send)
    for step in reversed(range(steps)):
        sum_a.gather(step, sum_b.send)
        sum_b.gather(step, sum_a.send)
        sum_a.placed(step)
        if step:
            sum_b.placed(step, sum_a.whole)
    grad_own = (to_self + halo_one.astype(F32) + halo_two.astype(F32)).astype(BF)
    on_second = masks[0][None, None] == 1

    def both_blocks(own):
        other = swap_cores(own)
        return jnp.where(on_second, jnp.stack([other, own]), jnp.stack([own, other]))

    mixed = both_blocks(mixed_own)
    grad_table = both_blocks(grad_own)
    grad_value, lines = (part.astype(F32) for part in sum_a.parts)
    grad_out = jnp.concatenate([lines[:cols], lines[cols:]], 1)
    sum_b.placed(0, grad_value, grad_out)
    grad_query, grad_key = (part.astype(F32) for part in sum_b.parts)
    return (mixed, grad_table, grad_query, grad_key, grad_value, grad_out)


def solution(mesh):
    return jax.shard_map(
        shards,
        mesh=mesh,
        in_specs=(
            P(None, "tm", None),
            P(None, "tm", None),
            P(None, "tm"),
            P(None, "tm"),
            P(None, "rep"),
            P(None, "rep"),
            P(None, "rep"),
            P("rep", None),
            P("rep"),
        ),
        out_specs=(
            P(None, "tm", None),
            P(None, "tm", None),
            P(None, "rep"),
            P(None, "rep"),
            P(None, "rep"),
            P("rep", None),
        ),
        check_vma=False,
    )
```

```python
import functools
import math

import jax
import jax.numpy as jnp
from jax import lax
from jax.experimental import pallas as pl
from jax.experimental.pallas import tpu as pltpu
from jax.sharding import PartitionSpec as P

HD = 128
BF = jnp.bfloat16
F32 = jnp.float32
AXES = ("tm", "rep")
LOG2E = math.log2(math.e)
DOWN = ((0,), (0,))
ACROSS = ((1,), (1,))


def dot(a, b, dims=((1,), (0,))):
    return lax.dot_general(a, b, (dims, ((), ())), preferred_element_type=F32)


def swap_cores(x):
    return lax.ppermute(x, "rep", [(0, 1), (1, 0)])


def shift_blocks(x, distance):
    n = lax.axis_size("tm")

    def worker(b):
        return 2 * b if b < n else 2 * (2 * n - 1 - b) + 1

    route = [(worker(b), worker((b + distance) % (2 * n))) for b in range(2 * n)]
    return lax.ppermute(x, AXES, route)


def bit_orders():
    bits = lax.axis_size("tm").bit_length() - 1
    count = min(3, bits)
    first = list(range(count))
    return first[1:] + first[:1], first, list(range(count, bits))


def partners(bit0, bit1):
    n = lax.axis_size("tm")
    pairs = []
    for i in range(n):
        pairs += [(2 * i, 2 * (i ^ (1 << bit0))), (2 * i + 1, 2 * (i ^ (1 << bit1)) + 1)]
    return pairs


def my_bits(orders):
    index = lax.axis_index("tm")
    on_first = lax.axis_index("rep") == 0
    return [jnp.where(on_first, (index >> a) & 1, (index >> b) & 1) for a, b in zip(*orders[:2])]


def tied(x, *others):
    return lax.optimization_barrier((x, *others))[0]


def call(kernel, name, outs, args, smem=1, far_in=0, scratch=(), limit=20, work=1):
    spaces = [pltpu.SMEM] * smem + [pl.ANY] * far_in + [pltpu.VMEM] * (len(args) - smem - far_in)
    return pl.pallas_call(
        kernel,
        in_specs=[pl.BlockSpec(memory_space=space) for space in spaces],
        out_specs=[pl.BlockSpec(memory_space=pltpu.VMEM)] * len(outs),
        out_shape=[jax.ShapeDtypeStruct(shape, dtype) for shape, dtype in outs],
        scratch_shapes=[pltpu.VMEM(shape, dtype) for shape, dtype in scratch]
        + ([pltpu.SemaphoreType.DMA((far_in,))] if far_in else []),
        compiler_params=pltpu.CompilerParams(vmem_limit_bytes=limit << 20),
        cost_estimate=pl.CostEstimate(flops=work << 27, bytes_accessed=work << 17, transcendentals=0),
        name=name,
    )(*args[:smem], *(pltpu.with_memory_space_constraint(x, pltpu.HBM) for x in args[smem : smem + far_in]), *args[smem + far_in :])


CORE, WINDOW, BITS = 0, 1, 2


def places_kernel(info, starts_ref, parcel_ref, shut_ref, masks_ref):
    del parcel_ref
    blk, keys = shut_ref.shape
    core = info[CORE]
    first = jnp.where(core == 0, starts_ref[0:1], starts_ref[1:2]) - info[WINDOW]
    first = jnp.transpose(jnp.broadcast_to(first, (8, blk)))[:, :1]
    at_key = lax.broadcasted_iota(jnp.int32, (blk, keys), 1)
    at_row = lax.broadcasted_iota(jnp.int32, (blk, keys), 0) + (keys - blk)
    shut_ref[...] = jnp.where((at_key >= first) & (at_key <= at_row), 0.0, -1e30)
    at = lax.broadcasted_iota(jnp.int32, masks_ref.shape, 0)
    masks = jnp.where(at == 0, core, 0)
    for step in range(info.shape[0] - BITS):
        masks = jnp.where(at == step + 1, info[BITS + step], masks)
    masks_ref[...] = masks


def before_kernel(
    info, wq_ref, wk_ref, wv_ref, wo_ref, cotangent_ref, wq_other_ref, wk_other_ref, wv_other_ref, wo_other_ref, x_ref,
    q_ref, k_ref, v_ref, g_attn_ref, g_ref, wq_all_ref, wk_all_ref, wv_all_ref, wo_all_ref, sems,
):
    blk, width = q_ref.shape
    cols = width // 2
    core = info[CORE]
    moves = [
        (wq_ref, wq_all_ref.at[:, :cols]),
        (wk_ref, wk_all_ref.at[:, :cols]),
        (wv_ref, wv_all_ref.at[:, :cols]),
        (wo_ref, wo_all_ref.at[:cols]),
        (cotangent_ref.at[core], g_ref),
    ]
    copies = [pltpu.make_async_copy(a, b, sems.at[i]) for i, (a, b) in enumerate(moves)]
    for copy in copies:
        copy.start()
    wq_all_ref[:, cols:] = wq_other_ref[...]
    wk_all_ref[:, cols:] = wk_other_ref[...]
    wv_all_ref[:, cols:] = wv_other_ref[...]
    wo_all_ref[cols:] = wo_other_ref[...]
    for i, (all_ref, out_ref) in enumerate(((wq_all_ref, q_ref), (wk_all_ref, k_ref), (wv_all_ref, v_ref))):
        copies[i].wait()
        out_ref[...] = dot(x_ref[:blk], all_ref[...]).astype(BF)
    for copy in copies[3:]:
        copy.wait()
    g_attn_ref[...] = dot(g_ref[...], wo_all_ref[...], ACROSS).astype(BF)


def softmax_parts(scores):
    weights = jnp.exp2(scores - jnp.max(scores, -1, keepdims=True))
    return weights * (1.0 / jnp.sum(weights, -1, keepdims=True))


def stamps_of(parcel_ref, blk):
    pieces = parcel_ref[blk:, :blk].astype(F32)
    at = lax.broadcasted_iota(jnp.int32, pieces.shape, 0)
    unit = jnp.where(at == 0, 1.0, jnp.where(at == 1, 256.0, jnp.where(at == 2, 65536.0, 0.0)))
    return jnp.sum(pieces * unit, 0, keepdims=True)


def window_terms(xs, ref, columns, scale):
    blk = ref.shape[0] // len(xs)
    parts = [dot(x[:blk], ref[i * blk : (i + 1) * blk, columns], DOWN) for i, x in enumerate(xs)]
    return functools.reduce(jnp.add, parts) * scale


def forward_kernel(
    scale, decay_ref, decay_other_ref, x_ref, one_ref, two_ref, q_ref, k_ref, v_ref, g_attn_ref, g_ref, wk_ref, wv_ref, shut_ref,
    probs_ref, k_win_ref, v_win_ref, away_ref, here_ref, o_ref, dv_ref,
):
    blk, width = q_ref.shape
    cols = width // 2
    k_win_ref[2 * blk :] = k_ref[...]
    v_win_ref[2 * blk :] = v_ref[...]
    xs = (two_ref, one_ref, x_ref)
    for i, ref in enumerate(xs[:2]):
        rows = slice(i * blk, (i + 1) * blk)
        k_win_ref[rows] = dot(ref[:blk], wk_ref[...]).astype(BF)
        v_win_ref[rows] = dot(ref[:blk], wv_ref[...]).astype(BF)
    times = [stamps_of(x, blk) for x in xs]
    gap = (times[2][:, blk - 1 :] - jnp.concatenate(times, 1)) * LOG2E
    heads = width // HD
    lanes = [slice(head * HD, (head + 1) * HD) for head in range(heads)]

    def scores_of(head):
        c = lanes[head]
        return dot(q_ref[:, c], k_win_ref[:, c], ACROSS)

    ahead = scores_of(0)
    low = None
    for head in range(heads + 1):
        scores = ahead
        if head + 1 < heads:
            ahead = scores_of(head + 1)
        before = low
        if head < heads:
            decay = decay_ref[head] if head < heads // 2 else decay_other_ref[head - heads // 2]
            probs = softmax_parts(scores * (LOG2E / math.sqrt(HD)) + (shut_ref[...] - gap * decay))
            probs_ref[head] = probs
            low = probs.astype(BF)
        if head:
            c = lanes[head - 1]
            o_ref[:, c] = dot(before, v_win_ref[:, c]).astype(BF)
            dv_ref[:, c] = dot(before, g_attn_ref[:, c], DOWN).astype(BF)
    for out_ref, lo in ((here_ref, 0), (away_ref, cols)):
        c = slice(lo, lo + cols)
        out_ref[:width] = window_terms(xs, dv_ref, c, scale)
        out_ref[width : width + cols] = dot(o_ref[:, c], g_ref[:, :cols], DOWN) * scale
        out_ref[width + cols :] = dot(o_ref[:, c], g_ref[:, cols:], DOWN) * scale


def backward_kernel(
    scale, x_ref, one_ref, two_ref, q_ref, k_win_ref, v_win_ref, g_attn_ref, probs_ref,
    away_ref, here_ref, dq_ref, dk_ref,
):
    width = q_ref.shape[1]
    cols = width // 2
    inv_scale = 1.0 / math.sqrt(HD)
    heads = width // HD
    lanes = [slice(head * HD, (head + 1) * HD) for head in range(heads)]

    def d_probs_of(head):
        return dot(g_attn_ref[:, lanes[head]], v_win_ref[:, lanes[head]], ACROSS)

    ahead = d_probs_of(0)
    d_scores = None
    for head in range(heads + 1):
        d_probs = ahead
        if head + 1 < heads:
            ahead = d_probs_of(head + 1)
        if head:
            c = lanes[head - 1]
            dq_ref[:, c] = (dot(d_scores, k_win_ref[:, c]) * inv_scale).astype(BF)
            dk_ref[:, c] = (dot(d_scores, q_ref[:, c], DOWN) * inv_scale).astype(BF)
        if head < heads:
            probs = probs_ref[head]
            delta = jnp.sum(probs * d_probs, -1, keepdims=True)
            d_scores = (probs * (d_probs - delta)).astype(BF)
    for out_ref, lo in ((here_ref, 0), (away_ref, cols)):
        c = slice(lo, lo + cols)
        out_ref[:width] = window_terms((x_ref,), dq_ref, c, scale)
        out_ref[width:] = window_terms((two_ref, one_ref, x_ref), dk_ref, c, scale)


def tail_kernel(
    dk_ref, wk_ref, dv_ref, wv_ref, dq_ref, wq_ref, o_ref, wo_ref, two_ref, one_ref, own_ref, mixed_ref
):
    blk = o_ref.shape[0]
    for i, out_ref in enumerate((two_ref, one_ref, own_ref)):
        rows = slice(i * blk, (i + 1) * blk)
        part = dot(dk_ref[rows], wk_ref[...], ACROSS) + dot(dv_ref[rows], wv_ref[...], ACROSS)
        if out_ref is own_ref:
            part += dot(dq_ref[...], wq_ref[...], ACROSS)
        out_ref[...] = part.astype(out_ref.dtype)
    mixed_ref[...] = dot(o_ref[...], wo_ref[...]).astype(BF)


class Summed:
    def __init__(self, masks, orders, here, away):
        self.masks = masks
        self.orders, self.rest = orders[:2], orders[2]
        self.keep, self.got = here, swap_cores(away)

    def passed(self, step, x):
        return lax.ppermute(x, AXES, partners(*(order[step] for order in self.orders)))

    def halve(self, step, *after):
        self.got = tied(self.got, *after)
        half = self.keep.shape[0] // 2
        second = self.masks[step, : self.keep.shape[1]][None] == 1

        def total(rows):
            return self.keep[rows] + self.got[rows].astype(F32)

        lower, upper = total(slice(None, half)), total(slice(half, None))
        self.keep = jnp.where(second, upper, lower)
        self.send = jnp.where(second, lower, upper).astype(BF)
        self.got = self.passed(step, self.send)

    def exchange(self, *after):
        total = self.keep + tied(self.got, *after).astype(F32)
        for bit in self.rest:
            self.send = total.astype(BF)
            got = lax.ppermute(self.send, AXES, partners(bit, bit))
            total = self.send.astype(F32) + got.astype(F32)
        self.whole = total.astype(BF)

    def gather(self, step, *after):
        self.send = self.whole = tied(self.whole, *after)
        self.got = self.passed(step, self.whole)

    def placed(self, step, *after):
        got = tied(self.got, *after)
        second = self.masks[step, : self.keep.shape[1]][None] == 1
        self.parts = jnp.where(second, got, self.whole), jnp.where(second, self.whole, got)
        self.whole = jnp.concatenate(self.parts, 0)


def shards(table, cotangent, stamps, starts, w_query, w_key, w_value, w_out, decay):
    n = lax.axis_size("tm")
    index = lax.axis_index("tm")
    core = lax.axis_index("rep")
    blk = table.shape[1]
    width = table.shape[2]
    cols = w_query.shape[1]
    block = jnp.where(core == 0, index, 2 * n - 1 - index)
    orders = bit_orders()
    info = jnp.stack([core, (block - 2) * blk, *my_bits(orders)]).astype(jnp.int32)

    x_own = lax.dynamic_index_in_dim(table, core, 0, False)
    t_own = lax.dynamic_index_in_dim(stamps, core, 0, False)
    pieces = jnp.stack([t_own & 255, (t_own >> 8) & 255, t_own >> 16]).astype(BF)
    pieces = jnp.pad(pieces, ((0, 13), (0, width - blk)))
    parcel = jnp.concatenate([x_own, pieces], 0)
    back_one = shift_blocks(parcel, 1)
    back_two = shift_blocks(parcel, 2)


    rows = ((blk, width), BF)
    window = ((3 * blk, width), BF)
    square = ((width, width), BF)
    pair = ((2 * width, cols), F32)
    heads = ((width // HD, blk, 3 * blk), F32)
    scale = 1.0 / math.sqrt(2 * blk * n)

    shut, masks = call(
        places_kernel, "places", [((blk, 3 * blk), F32), ((8, width), jnp.int32)], (info, starts, parcel), work=0
    )
    others = [swap_cores(tied(x, parcel)) for x in (w_query, w_key, w_value, w_out, decay)]
    decay_other = others.pop()
    q, k_own, v_own, g_attn, g_own, wq, wk, wv, wo = call(
        before_kernel,
        "before",
        [rows, rows, rows, rows, rows, square, square, square, square],
        (info, w_query, w_key, w_value, w_out, cotangent, *others, parcel),
        far_in=5,
        work=0,
    )
    probs, k_win, v_win, away_a, here_a, attn, dv = call(
        functools.partial(forward_kernel, scale),
        "forward",
        [heads, window, window, pair, pair, rows, window],
        (decay, decay_other, parcel, back_one, back_two, q, k_own, v_own, g_attn, g_own, wk, wv, shut),
        smem=2,
        work=32,
    )
    sum_a = Summed(masks[1:], orders, here_a, away_a)
    away_b, here_b, dq, dk = call(
        functools.partial(backward_kernel, scale),
        "backward",
        [pair, pair, rows, window],
        (parcel, back_one, back_two, q, k_win, v_win, g_attn, probs),
        smem=0,
        work=24,
    )
    sum_b = Summed(masks[1:], orders, here_b, away_b)
    to_two, to_one, to_self, mixed_own = call(
        tail_kernel, "tail", [rows, rows, ((blk, width), F32), rows], (dk, wk, dv, wv, dq, wq, attn, wo), smem=0, work=8
    )
    steps = len(orders[0])
    for step in range(steps):
        sum_a.halve(step, *([sum_b.send] if step else []))
        sum_b.halve(step, sum_a.send)
        if step == min(1, steps - 1):
            halo_one = shift_blocks(tied(to_one, sum_b.send), -1)
        if step == steps - 1:
            halo_two = shift_blocks(tied(to_two, sum_b.send), -2)
    sum_a.exchange(sum_b.send)
    sum_b.exchange(sum_a.send)
    for step in reversed(range(steps)):
        sum_a.gather(step, sum_b.send)
        sum_b.gather(step, sum_a.send)
        sum_a.placed(step)
        if step:
            sum_b.placed(step, sum_a.whole)
    grad_own = (to_self + halo_one.astype(F32) + halo_two.astype(F32)).astype(BF)
    on_second = masks[0][None, None] == 1

    finished = jnp.concatenate([mixed_own, grad_own], 0)
    others = swap_cores(finished)

    def both_blocks(own, other):
        return jnp.where(on_second, jnp.stack([other, own]), jnp.stack([own, other]))

    mixed = both_blocks(mixed_own, others[:blk])
    grad_table = both_blocks(grad_own, others[blk:])
    grad_value, lines = (part.astype(F32) for part in sum_a.parts)
    grad_out = jnp.concatenate([lines[:cols], lines[cols:]], 1)
    sum_b.placed(0, grad_value, grad_out)
    grad_query, grad_key = (part.astype(F32) for part in sum_b.parts)
    return (mixed, grad_table, grad_query, grad_key, grad_value, grad_out)


def solution(mesh):
    return jax.shard_map(
        shards,
        mesh=mesh,
        in_specs=(
            P(None, "tm", None),
            P(None, "tm", None),
            P(None, "tm"),
            P(None, "tm"),
            P(None, "rep"),
            P(None, "rep"),
            P(None, "rep"),
            P("rep", None),
            P("rep"),
        ),
        out_specs=(
            P(None, "tm", None),
            P(None, "tm", None),
            P(None, "rep"),
            P(None, "rep"),
            P(None, "rep"),
            P("rep", None),
        ),
        check_vma=False,
    )
```
